32 devices in a mesh: grp: 8 (over z, y), lag: 4 (over x, core).
Axes of the slice: x: 2, y: 2, z: 4, core: 2. Of those that a mesh axis runs over, the one named last changes fastest.
Arguments:
- history: float32 [8, 256, 32, 128], P('lag', 'grp'), may hold values from -6 to 6
- tiles: bfloat16 [16384, 128, 128], P(('grp', 'lag')), may hold values from -0.015625 to 0.015625
- tile_src: int32 [16384], P(('grp', 'lag')), may hold values from 0 to 255
- tile_obs: int32 [16384], P(('grp', 'lag')), may hold values from 0 to 16
- tile_lag: int32 [16384], P(('grp', 'lag')), may hold values from 0 to 1
- incident: float32 [16, 32, 128], P('grp', 'lag'), may hold values from -6 to 6
- near_inverse: bfloat16 [16, 128, 128], P('grp'), may hold values from -0.5 to 0.5
Outputs:
- field: float32 [16, 32, 128], P('grp', 'lag')
- new_current: float32 [16, 32, 128], P('grp', 'lag')
The draws below stay inside these ranges and needn't reach their ends.
Inputs may be any that keep to these rules, and one draw needn't show every extreme that they name: `tile_obs`: a value of 16 marks a padded tile.
All inputs are finite; a program needn't handle non-finite values.
Results may differ from the reference program's by a relative error of at most 0.0035.
Values may be sent and summed in bfloat16 or wider, within the bound.
A program may use at most 128 MiB of HBM per device.

```python
import jax
import jax.numpy as jnp
from jax import lax

G = 128
A = 32
LAG_DEV = 2
TILES = 512
SRC = 256
OBS = 16
LAGS = 8
TILES_ALL = 16384
N_GRP = 8
N_LAG = 4


def set_ends(drawn, rng, smallest, top_value):
    longest = drawn.shape.index(max(drawn.shape))
    spots = []
    for shift in (0, 1):
        where = [jax.random.randint(jax.random.fold_in(rng, axis), (), 0, length) for axis, length in enumerate(drawn.shape)]
        where[longest] = (where[longest] + shift) % drawn.shape[longest]
        spots.append(tuple(where))
    return drawn.at[spots[0]].set(smallest).at[spots[1]].set(top_value)


def level_of(rng, shape, split, low, high):
    level = 1.0
    for dim, shards_of in split:
        steps = jax.random.uniform(jax.random.fold_in(jax.random.fold_in(rng, 6), dim), (shards_of,), jnp.float32, low / len(split), high / len(split))
        level = level * jnp.repeat(jnp.exp(steps), shape[dim] // shards_of).reshape((-1,) + (1,) * (len(shape) - 1 - dim))
    return level


def centred(rng, shape, deviation, reach, cuts=(), kind=jnp.bfloat16):
    array = deviation * jax.random.normal(rng, shape, jnp.float32)
    if cuts:
        array = array * level_of(rng, shape, cuts, -0.22, 0.18)
    return jnp.clip(array, -reach, reach).astype(kind)


def setup_inputs(seed: int = 0) -> dict:
    arg_keys = jax.random.split(jax.random.key(seed), 8)
    history = centred(arg_keys[0], (LAGS, SRC, A, G), 1.0, 6.0, ((0, 4), (1, 8)), jnp.float32)
    tiles = centred(arg_keys[1], (TILES_ALL, G, G), (G * TILES_ALL // OBS) ** -0.5, 0.015625, ((0, 32),))
    tile_src = set_ends(jax.random.randint(arg_keys[2], (TILES_ALL,), 0, SRC), jax.random.fold_in(arg_keys[2], 1), 0, SRC - 1).astype(jnp.int32)
    tile_obs = set_ends(jax.random.randint(arg_keys[3], (TILES_ALL,), 0, OBS + 1), jax.random.fold_in(arg_keys[3], 1), 0, OBS).astype(jnp.int32)
    tile_lag = set_ends(jax.random.randint(arg_keys[4], (TILES_ALL,), 0, LAG_DEV), jax.random.fold_in(arg_keys[4], 1), 0, LAG_DEV - 1).astype(jnp.int32)
    incident = centred(arg_keys[5], (OBS, A, G), 1.0, 6.0, ((0, 8), (1, 4)), jnp.float32)
    near_inverse = centred(arg_keys[6], (OBS, G, G), G ** -0.5, 0.5, ((0, 8),))
    return dict(history=history, tiles=tiles, tile_src=tile_src, tile_obs=tile_obs, tile_lag=tile_lag, incident=incident, near_inverse=near_inverse)


def reference(history, tiles, tile_src, tile_obs, tile_lag, incident, near_inverse):
    hist16 = history.astype(jnp.bfloat16)
    flat = hist16.reshape(LAGS * SRC, A, G)
    blocks = N_GRP * N_LAG

    def one_block(total, block):
        start = (block * TILES).astype(jnp.int32)
        part_tiles = lax.dynamic_slice_in_dim(tiles, start, TILES, 0)
        sources = lax.dynamic_slice_in_dim(tile_src, start, TILES, 0)
        targets = lax.dynamic_slice_in_dim(tile_obs, start, TILES, 0)
        lags = lax.dynamic_slice_in_dim(tile_lag, start, TILES, 0)
        global_lag = (block % N_LAG).astype(jnp.int32) * LAG_DEV + lags
        picked = flat[(global_lag * SRC + sources).astype(jnp.int32)]
        terms = jnp.einsum("kas,kos->kao", picked.astype(jnp.float32), part_tiles.astype(jnp.float32))
        return total + jax.ops.segment_sum(terms, targets, num_segments=OBS), None

    start_total = jnp.zeros((OBS, A, G), jnp.float32)
    field, _ = lax.scan(one_block, start_total, jnp.arange(blocks, dtype=jnp.int32))
    rhs = (incident - field).astype(jnp.bfloat16)
    new_current = jnp.einsum("oag,ohg->oah", rhs.astype(jnp.float32), near_inverse.astype(jnp.float32))
    return field, new_current
```

```python
import functools

import jax
import jax.numpy as jnp
from jax import lax
from jax.experimental import pallas as pl
from jax.experimental.pallas import tpu as pltpu
from jax.sharding import PartitionSpec as P

MIB = 1 << 20


def gather_kernel(n_slow, n_fast, chunks, early, hist_ref, out_ref, own, send_sem, recv_sem, local_sem):
    lags, per_dev = own.shape[0], own.shape[1]
    per_lag = chunks // lags
    size = per_dev // per_lag
    me = lax.axis_index("grp")
    z, y = me // n_fast, me % n_fast

    def place(column, c):
        return c // per_lag, (c % per_lag) * size

    def home(origin, c):
        lag, start = place(origin, c)
        return out_ref.at[lag, pl.ds(origin * per_dev + start, size)]

    def mine(c):
        lag, start = place(me, c)
        return own.at[lag, pl.ds(start, size)]

    def remote(src, origin, c, slot, target):
        return pltpu.make_async_remote_copy(
            src_ref=src,
            dst_ref=home(origin, c),
            send_sem=send_sem.at[origin, c, slot],
            recv_sem=recv_sem.at[origin, c],
            device_id={"grp": target},
            device_id_type=pl.DeviceIdType.MESH,
        )

    def wait_arrival(origin, c):
        remote(home(origin, c), origin, c, 0, me).wait_recv()

    def along(step, origin, c, src, drain):
        @pl.when((z + step >= 0) & (z + step < n_slow))
        def _():
            copy = remote(src, origin, c, 0 if step < 0 else 1, me + step * n_fast)
            copy.wait_send() if drain else copy.start()

    def across(origin, c, src, drain):
        for j in range(1, n_fast):
            copy = remote(src, origin, c, 1 + j, z * n_fast + (y + j) % n_fast)
            copy.wait_send() if drain else copy.start()

    def walk(drain):
        @pl.loop(0, chunks)
        def _(c):
            across(me, c, mine(c), drain)
            along(-1, me, c, mine(c), drain)
            along(1, me, c, mine(c), drain)

        for j in range(1, n_fast):
            peer = z * n_fast + (y + j) % n_fast
            for c in range(early):
                if not drain:
                    wait_arrival(peer, c)
                along(-1, peer, c, home(peer, c), drain)
                along(1, peer, c, home(peer, c), drain)

        for d in range(1, n_slow):

            @pl.loop(0, chunks)
            def _(c):
                for sign in (1, -1):

                    @pl.when((z + sign * d >= 0) & (z + sign * d < n_slow))
                    def _():
                        origin = me + sign * d * n_fast
                        if not drain:
                            wait_arrival(origin, c)
                        along(-sign, origin, c, home(origin, c), drain)

                        @pl.when(c >= early)
                        def _():
                            across(origin, c, home(origin, c), drain)

            for j in range(1, n_fast):
                for c in range(early):
                    for sign in (1, -1):

                        @pl.when((z + sign * d >= 0) & (z + sign * d < n_slow))
                        def _():
                            origin = (z + sign * d) * n_fast + (y + j) % n_fast
                            if not drain:
                                wait_arrival(origin, c)
                            along(-sign, origin, c, home(origin, c), drain)

    barrier = pltpu.get_barrier_semaphore()
    for step in (-1, 1):

        @pl.when((z + step >= 0) & (z + step < n_slow))
        def _():
            pl.semaphore_signal(
                barrier, inc=1, device_id={"grp": me + step * n_fast}, device_id_type=pl.DeviceIdType.MESH
            )

    for j in range(1, n_fast):
        pl.semaphore_signal(
            barrier, inc=1, device_id={"grp": z * n_fast + (y + j) % n_fast}, device_id_type=pl.DeviceIdType.MESH
        )
    own[...] = hist_ref[...].astype(own.dtype)
    pl.semaphore_wait(barrier, jnp.where(z > 0, 1, 0) + jnp.where(z < n_slow - 1, 1, 0) + n_fast - 1)

    kept = pltpu.make_async_copy(own, out_ref.at[:, pl.ds(me * per_dev, per_dev)], local_sem)
    kept.start()
    walk(False)
    for j in range(1, n_fast):
        column = (y + j) % n_fast
        for d in range(n_slow):
            origin = (z + d) % n_slow * n_fast + column

            @pl.loop(early, chunks)
            def _(c):
                wait_arrival(origin, c)

    kept.wait()
    walk(True)


def gather(history, n_grp):
    lags, per_dev, angles, width = history.shape
    n_slow = 4 if n_grp % 4 == 0 else 1
    n_fast = n_grp // n_slow
    chunks = lags * 4
    return pl.pallas_call(
        functools.partial(gather_kernel, n_slow, n_fast, chunks, 1),
        out_shape=jax.ShapeDtypeStruct((lags, n_grp * per_dev, angles, width), jnp.bfloat16),
        in_specs=[pl.BlockSpec(memory_space=pltpu.VMEM)],
        out_specs=pl.BlockSpec(memory_space=pl.ANY),
        scratch_shapes=[
            pltpu.VMEM(history.shape, jnp.bfloat16),
            pltpu.SemaphoreType.DMA((n_grp, chunks, 1 + n_fast)),
            pltpu.SemaphoreType.DMA((n_grp, chunks)),
            pltpu.SemaphoreType.DMA,
        ],
        compiler_params=pltpu.CompilerParams(collective_id=0, has_side_effects=True, vmem_limit_bytes=16 * MIB),
        name="gather",
    )(history)


def products_kernel(sources, unroll, src_ref, obs_ref, lag_ref, hist_ref, tiles_ref, out_ref, acc):
    block = tiles_ref.shape[0]
    step = pl.program_id(0)
    copies = acc.shape[0]
    observers = out_ref.shape[1]
    part = out_ref.shape[2]

    @pl.when(step == 0)
    def _():
        acc[...] = jnp.zeros_like(acc)

    @pl.loop(0, block // unroll)
    def _(i):
        for u in range(unroll):
            local = i * unroll + u
            r = step * block + local
            picked = hist_ref[lag_ref[r] * sources + src_ref[r]]
            term = lax.dot_general(
                picked, tiles_ref[local], (((1,), (1,)), ((), ())), preferred_element_type=jnp.float32
            )
            acc[u % copies, obs_ref[r]] += term

    @pl.when(step == pl.num_programs(0) - 1)
    def _():
        total = acc[0, :observers]
        for k in range(1, copies):
            total = total + acc[k, :observers]
        for j in range(out_ref.shape[0]):
            out_ref[j] = total[:, j * part : (j + 1) * part]


def products(gathered, tiles, tile_src, tile_obs, tile_lag, observers, n_lag):
    lags, sources, angles, width = gathered.shape
    count = tiles.shape[0]
    block = 64
    out = (n_lag, observers, angles // n_lag, width)
    return pl.pallas_call(
        functools.partial(products_kernel, sources, 16),
        out_shape=jax.ShapeDtypeStruct(out, jnp.float32),
        grid=(count // block,),
        in_specs=[pl.BlockSpec(memory_space=pltpu.SMEM)] * 3
        + [
            pl.BlockSpec((lags * sources, angles, width), lambda i: (0, 0, 0)),
            pl.BlockSpec((block, width, width), lambda i: (i, 0, 0)),
        ],
        out_specs=pl.BlockSpec(out, lambda i: (0, 0, 0, 0)),
        scratch_shapes=[pltpu.VMEM((4, observers + 1, angles, width), jnp.float32)],
        compiler_params=pltpu.CompilerParams(vmem_limit_bytes=48 * MIB),
        name="products",
    )(tile_src, tile_obs, tile_lag, gathered.reshape(lags * sources, angles, width), tiles)


def finish_kernel(
    n_grp, n_lag, partial_ref, incident_ref, near_ref, field_ref, current_ref, by_lag, summed, by_grp, send1, recv1, send2, recv2
):
    g, l = lax.axis_index("grp"), lax.axis_index("lag")
    mine = field_ref.shape[0]
    barrier = pltpu.get_barrier_semaphore()
    for axis, me, n in (("lag", l, n_lag), ("grp", g, n_grp)):
        for j in range(1, n):
            pl.semaphore_signal(
                barrier, inc=1, device_id={axis: (me + j) % n}, device_id_type=pl.DeviceIdType.MESH
            )
    pl.semaphore_wait(barrier, n_lag + n_grp - 2)

    copies = []
    for j in range(1, n_lag):
        target = (l + j) % n_lag
        copy = pltpu.make_async_remote_copy(
            src_ref=partial_ref.at[target],
            dst_ref=by_lag.at[j - 1],
            send_sem=send1.at[j - 1],
            recv_sem=recv1.at[j - 1],
            device_id={"lag": target},
            device_id_type=pl.DeviceIdType.MESH,
        )
        copy.start()
        copies.append(copy)
    total = partial_ref[l]
    for j, copy in enumerate(copies):
        copy.wait_recv()
        total = total + by_lag[j]
    summed[...] = total

    later = []
    for j in range(1, n_grp):
        target = (g + j) % n_grp
        copy = pltpu.make_async_remote_copy(
            src_ref=summed.at[pl.ds(target * mine, mine)],
            dst_ref=by_grp.at[j - 1],
            send_sem=send2.at[j - 1],
            recv_sem=recv2.at[j - 1],
            device_id={"grp": target},
            device_id_type=pl.DeviceIdType.MESH,
        )
        copy.start()
        later.append(copy)
    field = summed[pl.ds(g * mine, mine)]
    for j, copy in enumerate(later):
        copy.wait_recv()
        field = field + by_grp[j]
    field_ref[...] = field
    rhs = (incident_ref[...] - field).astype(jnp.bfloat16)
    for o in range(mine):
        current_ref[o] = lax.dot_general(
            rhs[o], near_ref[o], (((1,), (1,)), ((), ())), preferred_element_type=jnp.float32
        )
    for copy in copies + later:
        copy.wait_send()


def finish(partial, incident, near_inverse, n_grp):
    n_lag, observers, part, width = partial.shape
    shape = jax.ShapeDtypeStruct(incident.shape, jnp.float32)
    return pl.pallas_call(
        functools.partial(finish_kernel, n_grp, n_lag),
        out_shape=(shape, shape),
        in_specs=[pl.BlockSpec(memory_space=pltpu.VMEM)] * 3,
        out_specs=(pl.BlockSpec(memory_space=pltpu.VMEM),) * 2,
        scratch_shapes=[
            pltpu.VMEM((n_lag - 1, observers, part, width), jnp.float32),
            pltpu.VMEM((observers, part, width), jnp.float32),
            pltpu.VMEM((n_grp - 1,) + incident.shape, jnp.float32),
            pltpu.SemaphoreType.DMA((n_lag - 1,)),
            pltpu.SemaphoreType.DMA((n_lag - 1,)),
            pltpu.SemaphoreType.DMA((n_grp - 1,)),
            pltpu.SemaphoreType.DMA((n_grp - 1,)),
        ],
        compiler_params=pltpu.CompilerParams(collective_id=1, has_side_effects=True, vmem_limit_bytes=16 * MIB),
        name="finish",
    )(partial, incident, near_inverse)


def body(history, tiles, tile_src, tile_obs, tile_lag, incident, near_inverse):
    n_grp, n_lag = lax.axis_size("grp"), lax.axis_size("lag")
    observers = incident.shape[0] * n_grp
    gathered = gather(history, n_grp)
    partial = products(gathered, tiles, tile_src, tile_obs, tile_lag, observers, n_lag)
    return finish(partial, incident, near_inverse, n_grp)


def solution(mesh):
    return jax.shard_map(
        body,
        mesh=mesh,
        in_specs=(
            P("lag", "grp", None, None),
            P(("grp", "lag"), None, None),
            P(("grp", "lag")),
            P(("grp", "lag")),
            P(("grp", "lag")),
            P("grp", "lag", None),
            P("grp", None, None),
        ),
        out_specs=(P("grp", "lag", None), P("grp", "lag", None)),
        check_vma=False,
    )
```
